256 devices in a mesh: region: 16 (over z, x_lo), neuron: 16 (over x_hi, y, core).
Axes of the slice: x: 4 (x_hi: 2, x_lo: 2; x = x_hi * 2 + x_lo), y: 4, z: 8, core: 2. Of those that a mesh axis runs over, the one named last changes fastest.
Arguments:
- counts: bfloat16 [16, 20480, 4096], P('region', 'neuron'), may hold values from 0 to 3, as said below
- latents: bfloat16 [64, 4096], P(None, 'neuron'), may hold values from -5 to 5
- loadings: bfloat16 [16, 64, 20480], P('region', None, 'neuron'), may hold values from -0.75 to 0.75
- bias: float32 [16, 20480], P('region', 'neuron'), may hold values from -3 to 3
- delays: int32 [16, 64], P('region'), may hold values from 0 to 128
- recorded: int32 [16], P('region'), may hold values from 1024 to 4096, as said below
Outputs:
- grad_latents: float32 [64, 4096], P(None, 'neuron')
- grad_loadings: float32 [16, 64, 20480], P('region', None, 'neuron')
- grad_bias: float32 [16, 20480], P('region', 'neuron')
The draws below stay inside these ranges and needn't reach their ends.
Inputs may be any that keep to these rules, and one draw needn't show every extreme that they name: At least one region is recorded over all 4096 bins. `counts`: whole numbers.
All inputs are finite; a program needn't handle non-finite values.
Results may differ from the reference program's by a relative error of at most 0.0021.
Values may be sent and summed in bfloat16 or wider, within the bound.
A program may use at most 64 MiB of HBM per device.

```python
import jax
import jax.numpy as jnp
from jax import lax

L = 64
REGIONS = 16
NEURONS = 20480
TIME = 4096
DELAY_MAX = 128


def draw_recorded(key, part):
    first_key, second_key = jax.random.split(jax.random.fold_in(key, 17))
    full = jax.random.randint(first_key, (), 0, REGIONS)
    spans = jax.random.randint(second_key, (REGIONS,), TIME // 4, TIME + 1)
    return jnp.where(jnp.arange(REGIONS) == full, TIME, spans).astype(jnp.int32)


def draw_counts(key, part):
    values = jax.random.randint(jax.random.fold_in(key, 29), (REGIONS, NEURONS, TIME), 0, 4)
    return values.astype(jnp.float32).astype(jnp.bfloat16)


def with_ends(drawn, own_key, smallest, largest):
    place = [jax.random.randint(jax.random.fold_in(own_key, axis), (), 0, length) for axis, length in enumerate(drawn.shape)]
    main_axis = drawn.shape.index(max(drawn.shape))
    next_to = place[:main_axis] + [(place[main_axis] + 1) % drawn.shape[main_axis]] + place[main_axis + 1:]
    return drawn.at[tuple(place)].set(smallest).at[tuple(next_to)].set(largest)


def block_scale(rng, extent, cuts, smallest, top_value):
    factor_of = 1.0
    for axis_at, parts in cuts:
        steps = jax.random.uniform(jax.random.fold_in(jax.random.fold_in(rng, 6), axis_at), (parts,), jnp.float32, smallest / len(cuts), top_value / len(cuts))
        factor_of = factor_of * jnp.repeat(jnp.exp(steps), extent[axis_at] // parts).reshape((-1,) + (1,) * (len(extent) - 1 - axis_at))
    return factor_of


def normal_values(stream_key, shape, width, most, cuts=(), kind=jnp.bfloat16):
    result = jax.random.normal(stream_key, shape, jnp.float32) * width
    if len(cuts) > 0:
        result = block_scale(stream_key, shape, cuts, -0.22, 0.18) * result
    return jnp.clip(result, min=-most, max=most).astype(kind)


def setup_inputs(seed: int = 0) -> dict:
    seeds = jax.random.split(jax.random.key(seed), 7)
    counts = draw_counts(jax.random.fold_in(seeds[6], 71), 0)
    latents = normal_values(seeds[1], (L, TIME), 1.0, 5.0, ((1, 16),))
    loadings = normal_values(seeds[2], (REGIONS, L, NEURONS), L ** -0.5, 0.75, ((0, 16), (2, 16)))
    bias = normal_values(seeds[3], (REGIONS, NEURONS), 0.5, 3.0, ((0, 16), (1, 16)), jnp.float32)
    delays = with_ends(jax.random.randint(seeds[4], (REGIONS, L), 0, DELAY_MAX + 1), jax.random.fold_in(seeds[4], 1), 0, DELAY_MAX).astype(jnp.int32)
    recorded = draw_recorded(jax.random.fold_in(seeds[6], 71), 0)
    return dict(counts=counts, latents=latents, loadings=loadings, bias=bias, delays=delays, recorded=recorded)


def delay_rows(source, delay_row, offset, span):
    def one_row(row, delay):
        return lax.dynamic_slice_in_dim(row, (offset - delay).astype(jnp.int32), span)
    return jax.vmap(one_row)(source, delay_row)


def advance_rows(source, delay_row, span):
    def one_row(row, delay):
        return lax.dynamic_slice_in_dim(row, delay.astype(jnp.int32), span)
    return jax.vmap(one_row)(source, delay_row)


def reference(counts, latents, loadings, bias, delays, recorded):
    padded = jnp.pad(latents, ((0, 0), (DELAY_MAX, 0)))

    def one_region(items):
        count_rows, load, bias_row, delay_row, length = items
        shifted = delay_rows(padded, delay_row, DELAY_MAX, TIME)
        eta = jnp.dot(load.T, shifted, preferred_element_type=jnp.float32) + bias_row[:, None]
        bins = jnp.arange(TIME, dtype=jnp.int32)
        resid = jnp.where((bins < length)[None, :], jnp.exp(eta) - count_rows.astype(jnp.float32), 0.0)
        resid_low = resid.astype(jnp.bfloat16)
        grad_load = jnp.dot(shifted, resid_low.T, preferred_element_type=jnp.float32)
        grad_bias = jnp.sum(resid, axis=1)
        grad_shift = jnp.dot(load, resid_low, preferred_element_type=jnp.float32)
        extended = jnp.pad(grad_shift, ((0, 0), (0, DELAY_MAX)))
        return grad_load, grad_bias, advance_rows(extended, delay_row, TIME)

    grad_load, grad_bias, moved = lax.map(one_region, (counts, loadings, bias, delays, recorded))
    return jnp.sum(moved, axis=0), grad_load, grad_bias
```

```python
import functools

import jax
import jax.numpy as jnp
from jax import lax
from jax.experimental import pallas as pl
from jax.experimental.pallas import tpu as pltpu
from jax.sharding import PartitionSpec as P

MESH = pl.DeviceIdType.MESH
LANES = 128
LAT = 64
NEU = 1280
TIME = 4096
TILES = TIME // LANES
CHIPS = 8
CHUNK = CHIPS * LANES
DEPTH = 128
ROWS = 4
F32 = jnp.float32
BF16 = jnp.bfloat16


def split_three(value):
    high = value.astype(BF16)
    rest = value - high.astype(F32)
    middle = rest.astype(BF16)
    return high.astype(F32), middle.astype(F32), rest - middle.astype(F32)


def kernel(
    counts_hbm, lat_ref, load_ref, bias_ref, delay_ref, rec_ref,
    out_lat, out_load, out_bias,
    counts, latb, rot, piece, load_t, bias_sum, spun, part, mate_in, pair, plane_in, mine, final_in,
    cnt_sem, ag_send, ag_recv, fw_send, fw_recv, a_send, a_recv, b_send, b_recv, c_send, c_recv,
):
    region = lax.axis_index("region")
    neuron = lax.axis_index("neuron")
    z, x_lo = region // 2, region % 2
    x_hi, y, core = neuron // 8, (neuron // 2) % 4, neuron % 2
    chip = neuron // 2
    x = x_hi * 2 + x_lo
    mate = (region, chip * 2 + 1 - core)

    block = NEU // ROWS
    loads = []
    for k in range(ROWS):
        rows = pl.ds(k * block, block)
        copy = pltpu.make_async_copy(counts_hbm.at[rows], counts.at[rows], cnt_sem.at[k])
        copy.start()
        loads.append(copy)

    plane = []
    for dx in range(4):
        for dy in range(4):
            if (dx, dy) != (0, 0):
                px, py = (x + dx) % 4, (y + dy) % 4
                plane.append(((z * 2 + px % 2), (px // 2) * 4 + py, px % 2))
    spread = []
    for dz in (0, 1, 7, 2, 6, 3, 5, 4):
        for dl in range(2):
            if (dz, dl) != (0, 0):
                spread.append((((z + dz) % 8), (x_lo + dl) % 2))

    barrier = pltpu.get_barrier_semaphore()
    pl.semaphore_signal(barrier, inc=1, device_id=mate, device_id_type=MESH)
    for reg, pos, _ in plane:
        pl.semaphore_signal(barrier, inc=1, device_id=(reg, pos * 2 + core), device_id_type=MESH)
    for pz, pl_lo in spread[1:]:
        pl.semaphore_signal(barrier, inc=1, device_id=(pz * 2 + pl_lo, neuron), device_id_type=MESH)
    pl.semaphore_wait(barrier, 1 + len(plane) + len(spread) - 1)

    sends = []

    def to_mate(source, pos):
        copy = pltpu.make_async_remote_copy(
            src_ref=source, dst_ref=latb.at[core, pos], send_sem=fw_send.at[pos], recv_sem=fw_recv.at[pos],
            device_id=mate, device_id_type=MESH,
        )
        copy.start()
        return copy

    arrivals = []
    for dxh, dy in ((0, 1), (0, 3), (1, 0), (0, 2), (1, 1), (1, 3), (1, 2)):
        px = 3 - x if dxh else x
        pos = (px // 2) * 4 + (y + dy) % 4
        copy = pltpu.make_async_remote_copy(
            src_ref=lat_ref, dst_ref=latb.at[core, chip], send_sem=ag_send.at[pos], recv_sem=ag_recv.at[chip],
            device_id=(z * 2 + px % 2, pos * 2 + core), device_id_type=MESH,
        )
        copy.start()
        sends.append(copy)
        arrivals.append(pos)
    sends.append(to_mate(lat_ref, chip))
    latb[core, chip] = lat_ref[...]

    ba, bb, bc = split_three(bias_ref[...])
    stacked = jnp.concatenate([load_ref[...].astype(F32), ba, bb, bc, jnp.zeros((DEPTH - LAT - 3, NEU), F32)], axis=0)
    load_t[...] = jnp.transpose(stacked).astype(BF16)
    tail = lax.broadcasted_iota(jnp.int32, (DEPTH - LAT, CHUNK), 0)
    piece[LAT:] = jnp.where(tail < 3, 1.0, 0.0).astype(BF16)
    out_load[...] = jnp.zeros_like(out_load)
    bias_sum[...] = jnp.zeros_like(bias_sum)
    rot[0] = jnp.zeros((LAT, LANES), F32)
    spun[TILES] = jnp.zeros((LAT, LANES), F32)
    same = lax.broadcasted_iota(jnp.int32, (LAT, LAT), 0) == lax.broadcasted_iota(jnp.int32, (LAT, LAT), 1)
    delay = jnp.sum(jnp.where(same, delay_ref[...].astype(F32), 0.0), axis=1, keepdims=True).astype(jnp.int32)
    lane = lax.broadcasted_iota(jnp.int32, (LAT, LANES), 1)
    back = (lane - delay) & (LANES - 1)
    ahead = (lane + delay) & (LANES - 1)
    kept = lane >= delay
    near = lane + delay < LANES
    recorded = rec_ref[0]

    for pos in arrivals:
        pltpu.make_async_copy(lat_ref, latb.at[core, pos], ag_recv.at[pos]).wait()
        sends.append(to_mate(latb.at[core, pos], pos))
    for pos in [chip] + arrivals:
        pltpu.make_async_copy(lat_ref, latb.at[1 - core, pos], fw_recv.at[pos]).wait()

    for tile in range(TILES):
        source = latb[(tile // 2) % 2, tile // 4, :, (tile % 2) * LANES : (tile % 2 + 1) * LANES]
        rot[tile + 1] = jnp.take_along_axis(source.astype(F32), back, axis=1)
    for copy in loads:
        copy.wait()

    def reduce_cores(group):
        def fill(pos, carry):
            for owner in range(2):
                kind = (0, 3)[owner] if group == 0 else (1, 2)[owner]
                tile = pos * 4 + kind
                part[group, owner, pos] = jnp.where(near, spun[tile], spun[tile + 1])
            return carry

        lax.fori_loop(0, CHIPS, fill, 0)
        copy = pltpu.make_async_remote_copy(
            src_ref=part.at[group, 1 - core], dst_ref=mate_in.at[group], send_sem=a_send.at[group],
            recv_sem=a_recv.at[group], device_id=mate, device_id_type=MESH,
        )
        copy.start()
        return copy

    def reduce_plane(group, waiting):
        waiting.wait_recv()
        for pos in range(CHIPS):
            total = part[group, core, pos] + mate_in[group, pos]
            pair[group, 2 * pos] = total[: LAT // 2]
            pair[group, 2 * pos + 1] = total[LAT // 2 :]
        me = chip * 2 + x_lo
        copies = []
        for k, (reg, pos, lo) in enumerate(plane):
            copy = pltpu.make_async_remote_copy(
                src_ref=pair.at[group, pos * 2 + lo], dst_ref=plane_in.at[group, me], send_sem=b_send.at[group, k],
                recv_sem=b_recv.at[group, me], device_id=(reg, pos * 2 + core), device_id_type=MESH,
            )
            copy.start()
            copies.append(copy)
        plane_in[group, me] = pair[group, me]
        return copies

    def reduce_region(group):
        for _, pos, lo in plane:
            pltpu.make_async_copy(pair.at[group, 0], plane_in.at[group, pos * 2 + lo], b_recv.at[group, pos * 2 + lo]).wait()
        total = plane_in[group, 0]
        for k in range(1, 2 * CHIPS):
            total = total + plane_in[group, k]
        mine[group] = total
        copies = []
        for k, (pz, lo) in enumerate(spread):
            copy = pltpu.make_async_remote_copy(
                src_ref=mine.at[group], dst_ref=final_in.at[group, region], send_sem=c_send.at[group, k],
                recv_sem=c_recv.at[group, region], device_id=(pz * 2 + lo, neuron), device_id_type=MESH,
            )
            copy.start()
            copies.append(copy)
        final_in[group, region] = total
        return copies

    def finish(group):
        for pz, lo in spread:
            pltpu.make_async_copy(mine.at[group], final_in.at[group, pz * 2 + lo], c_recv.at[group, pz * 2 + lo]).wait()
        start = pl.multiple_of((core if group == 0 else 1 - core) * LANES, LANES)
        for lo in range(2):
            total = final_in[group, lo]
            for k in range(1, 8):
                total = total + final_in[group, 2 * k + lo]
            out_lat[lo * (LAT // 2) : (lo + 1) * (LAT // 2), pl.ds(start, LANES)] = total

    def chunk(step, carry):
        kind = (5 - step) % 4
        for pos in range(CHIPS):
            tile = pos * 4 + kind
            piece[:LAT, pos * LANES : (pos + 1) * LANES] = jnp.where(kept, rot[tile + 1], rot[tile]).astype(BF16)
        bins = lax.broadcasted_iota(jnp.int32, (1, CHUNK), 1)
        bins = (bins // LANES) * (4 * LANES) + kind * LANES + bins % LANES
        eta = jnp.dot(load_t[...], piece[...], preferred_element_type=F32)
        observed = jnp.concatenate(
            [counts[:, pl.ds(pl.multiple_of((pos * 4 + kind) * LANES, LANES), LANES)] for pos in range(CHIPS)], axis=1
        )
        resid = jnp.where(bins < recorded, jnp.exp(eta) - observed.astype(F32), 0.0)
        total = resid[:, :LANES]
        for pos in range(1, CHIPS):
            total = total + resid[:, pos * LANES : (pos + 1) * LANES]
        bias_sum[...] += total
        low = resid.astype(BF16)
        out_load[...] += lax.dot_general(piece[:LAT], low, (((1,), (1,)), ((), ())), preferred_element_type=F32)
        shift = jnp.dot(load_ref[...], low, preferred_element_type=F32)
        for pos in range(CHIPS):
            spun[pos * 4 + kind] = jnp.take_along_axis(shift[:, pos * LANES : (pos + 1) * LANES], ahead, axis=1)
        return carry

    lax.fori_loop(0, 3, chunk, 0)
    first = reduce_cores(0)
    lax.fori_loop(3, 4, chunk, 0)
    second = reduce_cores(1)
    sends += [first, second]
    sends += reduce_plane(0, first)
    sends += reduce_plane(1, second)
    out_bias[...] = jnp.sum(jnp.transpose(bias_sum[...]), axis=0, keepdims=True)
    sends += reduce_region(0)
    sends += reduce_region(1)
    finish(0)
    finish(1)
    for copy in sends:
        copy.wait_send()


def per_device(counts, latents, loadings, bias, delays, recorded):
    vmem = pl.BlockSpec(memory_space=pltpu.VMEM)
    half = (LAT // 2, LANES)
    grad_lat, grad_load, grad_bias = pl.pallas_call(
        kernel,
        out_shape=(
            jax.ShapeDtypeStruct((LAT, 2 * LANES), F32),
            jax.ShapeDtypeStruct((LAT, NEU), F32),
            jax.ShapeDtypeStruct((1, NEU), F32),
        ),
        in_specs=[pl.BlockSpec(memory_space=pl.ANY), vmem, vmem, vmem, vmem, pl.BlockSpec(memory_space=pltpu.SMEM)],
        out_specs=(vmem, vmem, vmem),
        scratch_shapes=[
            pltpu.VMEM((NEU, TIME), BF16),
            pltpu.VMEM((2, CHIPS, LAT, 2 * LANES), BF16),
            pltpu.VMEM((TILES + 1, LAT, LANES), F32),
            pltpu.VMEM((DEPTH, CHUNK), BF16),
            pltpu.VMEM((NEU, DEPTH), BF16),
            pltpu.VMEM((NEU, LANES), F32),
            pltpu.VMEM((TILES + 1, LAT, LANES), F32),
            pltpu.VMEM((2, 2, CHIPS, LAT, LANES), F32),
            pltpu.VMEM((2, CHIPS, LAT, LANES), F32),
            pltpu.VMEM((2, 2 * CHIPS) + half, F32),
            pltpu.VMEM((2, 2 * CHIPS) + half, F32),
            pltpu.VMEM((2,) + half, F32),
            pltpu.VMEM((2, 16) + half, F32),
            pltpu.SemaphoreType.DMA((ROWS,)),
            pltpu.SemaphoreType.DMA((CHIPS,)),
            pltpu.SemaphoreType.DMA((CHIPS,)),
            pltpu.SemaphoreType.DMA((CHIPS,)),
            pltpu.SemaphoreType.DMA((CHIPS,)),
            pltpu.SemaphoreType.DMA((2,)),
            pltpu.SemaphoreType.DMA((2,)),
            pltpu.SemaphoreType.DMA((2, 15)),
            pltpu.SemaphoreType.DMA((2, 16)),
            pltpu.SemaphoreType.DMA((2, 15)),
            pltpu.SemaphoreType.DMA((2, 16)),
        ],
        compiler_params=pltpu.CompilerParams(
            collective_id=0, has_side_effects=True, vmem_limit_bytes=58 * 2**20
        ),
    )(counts[0], latents, loadings[0], bias, delays, recorded)
    return grad_lat, grad_load[None], grad_bias


def solution(mesh):
    placed = (
        P("region", "neuron", None),
        P(None, "neuron"),
        P("region", None, "neuron"),
        P("region", "neuron"),
        P("region", None),
        P("region"),
    )
    return jax.shard_map(
        per_device,
        mesh=mesh,
        in_specs=placed,
        out_specs=(P(None, "neuron"), P("region", None, "neuron"), P("region", "neuron")),
        check_vma=False,
    )
```

```python
import functools

import jax
import jax.numpy as jnp
from jax import lax
from jax.experimental import pallas as pl
from jax.experimental.pallas import tpu as pltpu
from jax.sharding import PartitionSpec as P

MESH = pl.DeviceIdType.MESH
LANES = 128
LAT = 64
HALF = LAT // 2
NEU = 1280
TIME = 4096
TILES = TIME // LANES
CHIPS = 8
CHUNK = CHIPS * LANES
DEPTH = 128
ROWS = 4
BLOCK = 256
CODED = LAT + 16
BITS = 14
NEAR = ((0, 1), (0, 3), (1, 0), (0, 2), (1, 1), (1, 3), (1, 2))
F32 = jnp.float32
BF16 = jnp.bfloat16
I16 = jnp.int16


def split_three(value):
    high = value.astype(BF16)
    rest = value - high.astype(F32)
    middle = rest.astype(BF16)
    return high.astype(F32), middle.astype(F32), rest - middle.astype(F32)


def exponent_of(largest):
    return jnp.floor(jnp.log2(jnp.maximum(largest, 1e-30))) + 1.0


def encode(value, exponent):
    return jnp.round(value * jnp.exp2(BITS - exponent)).astype(jnp.int32).astype(I16)


def stamp(exponent):
    return jnp.broadcast_to(exponent, (CODED - LAT, LANES)).astype(jnp.int32).astype(I16)


def decode(ref, *index):
    whole = ref[index].astype(jnp.int32).astype(F32)
    return whole[:LAT] * jnp.exp2(whole[LAT : LAT + 1] - BITS)


def kernel(
    counts_hbm, lat_hbm, load_hbm, bias_hbm, delay_hbm, rec_ref,
    out_lat, out_load, out_bias,
    counts, load_ref, bias_ref, delay_ref, latb, rot, piece, load_t, bias_sum, spun, part, mate_in, pair, plane_in,
    mine, final_in, grad_lat, grad_load, grad_bias,
    in_sem, cnt_sem, ag_send, ag_recv, fw_send, fw_recv, a_send, a_recv, b_send, b_recv, c_send, c_recv, out_sem,
):
    region = lax.axis_index("region")
    neuron = lax.axis_index("neuron")
    z, x_lo = region // 2, region % 2
    x_hi, y, core = neuron // 8, (neuron // 2) % 4, neuron % 2
    chip = neuron // 2
    x = x_hi * 2 + x_lo
    mate = (region, chip * 2 + 1 - core)

    plane = []
    for dx in range(4):
        for dy in range(4):
            if (dx, dy) != (0, 0):
                px, py = (x + dx) % 4, (y + dy) % 4
                plane.append(((z * 2 + px % 2), (px // 2) * 4 + py, px % 2))
    spread = []
    for dz in (0, 4, 3, 5, 2, 6, 1, 7):
        for dl in (1, 0):
            if (dz, dl) != (0, 0):
                spread.append((((z + dz) % 8), (x_lo + dl) % 2))

    barrier = pltpu.get_barrier_semaphore()
    for pz, lo in spread[1:]:
        pl.semaphore_signal(barrier, inc=1, device_id=(pz * 2 + lo, neuron), device_id_type=MESH)
    for reg, pos, _ in plane:
        pl.semaphore_signal(barrier, inc=1, device_id=(reg, pos * 2 + core), device_id_type=MESH)
    pl.semaphore_signal(barrier, inc=1, device_id=mate, device_id_type=MESH)

    own = []
    for h in range(2):
        copy = pltpu.make_async_copy(
            lat_hbm.at[:, pl.ds(h * LANES, LANES)], latb.at[core, h, chip], in_sem.at[h]
        )
        copy.start()
        own.append(copy)
    smalls = []
    for k, (source, target) in enumerate(((load_hbm, load_ref), (bias_hbm, bias_ref), (delay_hbm, delay_ref))):
        copy = pltpu.make_async_copy(source, target, in_sem.at[2 + k])
        copy.start()
        smalls.append(copy)
    block = NEU // ROWS
    loads = []
    for k in range(ROWS):
        rows = pl.ds(k * block, block)
        copy = pltpu.make_async_copy(counts_hbm.at[rows], counts.at[rows], cnt_sem.at[k])
        copy.start()
        loads.append(copy)

    for copy in smalls:
        copy.wait()
    ba, bb, bc = split_three(bias_ref[...])
    stacked = jnp.concatenate([load_ref[...].astype(F32), ba, bb, bc, jnp.zeros((DEPTH - LAT - 3, NEU), F32)], axis=0)
    load_t[...] = jnp.transpose(stacked).astype(BF16)
    tail = lax.broadcasted_iota(jnp.int32, (DEPTH - LAT, CHUNK), 0)
    for kind in range(4):
        piece[kind, LAT:] = jnp.where(tail < 3, 1.0, 0.0).astype(BF16)
    grad_load[...] = jnp.zeros_like(grad_load)
    bias_sum[...] = jnp.zeros_like(bias_sum)
    rot[0] = jnp.zeros((LAT, LANES), F32)
    spun[TILES] = jnp.zeros((LAT, LANES), F32)
    same = lax.broadcasted_iota(jnp.int32, (LAT, LAT), 0) == lax.broadcasted_iota(jnp.int32, (LAT, LAT), 1)
    delay = jnp.sum(jnp.where(same, delay_ref[...].astype(F32), 0.0), axis=1, keepdims=True).astype(jnp.int32)
    lane = lax.broadcasted_iota(jnp.int32, (LAT, LANES), 1)
    back = (lane - delay) & (LANES - 1)
    ahead = (lane + delay) & (LANES - 1)
    kept = lane >= delay
    near = lane + delay < LANES
    recorded = rec_ref[...].reshape(1, 1)
    for copy in own:
        copy.wait()
    pl.semaphore_wait(barrier, 1 + len(plane) + len(spread) - 1)
    sends = []

    def to_mate(h, pos):
        copy = pltpu.make_async_remote_copy(
            src_ref=latb.at[core, h, pos], dst_ref=latb.at[core, h, pos], send_sem=fw_send.at[h, pos],
            recv_sem=fw_recv.at[h, pos], device_id=mate, device_id_type=MESH,
        )
        copy.start()
        sends.append(copy)

    arrivals = []
    for h in (core, 1 - core):
        for dxh, dy in NEAR:
            px = 3 - x if dxh else x
            pos = (px // 2) * 4 + (y + dy) % 4
            copy = pltpu.make_async_remote_copy(
                src_ref=latb.at[core, h, chip], dst_ref=latb.at[core, h, chip], send_sem=ag_send.at[h, pos],
                recv_sem=ag_recv.at[h, chip], device_id=(z * 2 + px % 2, pos * 2 + core), device_id_type=MESH,
            )
            copy.start()
            sends.append(copy)
            if len(arrivals) < CHIPS - 1:
                arrivals.append(pos)
        to_mate(h, chip)

    def pass_on(h):
        for pos in arrivals:
            pltpu.make_async_copy(latb.at[core, h, chip], latb.at[core, h, pos], ag_recv.at[h, pos]).wait()
            to_mate(h, pos)

    def from_mate(h):
        for pos in [chip] + arrivals:
            pltpu.make_async_copy(latb.at[core, h, chip], latb.at[1 - core, h, pos], fw_recv.at[h, pos]).wait()

    def rotate(kind):
        for pos in range(CHIPS):
            source = latb[kind // 2, kind % 2, pos].astype(F32)
            rot[pos * 4 + kind + 1] = jnp.take_along_axis(source, back, axis=1)

    pass_on(core)
    from_mate(1 - core)
    rotate(0)
    rotate(3)
    for copy in loads:
        copy.wait()

    def chunk(kind, between):
        for pos in range(CHIPS):
            tile = pos * 4 + kind
            piece[kind, :LAT, pos * LANES : (pos + 1) * LANES] = jnp.where(kept, rot[tile + 1], rot[tile]).astype(BF16)
        bins = lax.broadcasted_iota(jnp.int32, (1, CHUNK), 1)
        bins = (bins // LANES) * (4 * LANES) + kind * LANES + bins % LANES
        live = bins < recorded
        shift = None
        for k in range(NEU // BLOCK):
            if k in between:
                between[k]()
            rows = slice(k * BLOCK, (k + 1) * BLOCK)
            eta = jnp.dot(load_t[rows], piece[kind], preferred_element_type=F32)
            observed = jnp.concatenate(
                [counts[rows, (pos * 4 + kind) * LANES : (pos * 4 + kind + 1) * LANES] for pos in range(CHIPS)], axis=1
            )
            resid = jnp.where(live, jnp.exp(eta) - observed.astype(F32), 0.0)
            total = resid[:, :LANES]
            for pos in range(1, CHIPS):
                total = total + resid[:, pos * LANES : (pos + 1) * LANES]
            bias_sum[rows] += total
            low = resid.astype(BF16)
            grad_load[:, rows] += lax.dot_general(
                piece[kind, :LAT], low, (((1,), (1,)), ((), ())), preferred_element_type=F32
            )
            part_shift = jnp.dot(load_ref[:, rows], low, preferred_element_type=F32)
            shift = part_shift if shift is None else shift + part_shift
        for pos in range(CHIPS):
            spun[pos * 4 + kind] = jnp.take_along_axis(shift[:, pos * LANES : (pos + 1) * LANES], ahead, axis=1)

    def advance(kind):
        for pos in range(CHIPS):
            tile = pos * 4 + kind
            moved = jnp.where(near, spun[tile], spun[tile + 1])
            part[kind, pos, 0] = moved[:HALF]
            part[kind, pos, 1] = moved[HALF:]

    def to_owner(kind):
        return pltpu.make_async_remote_copy(
            src_ref=part.at[kind], dst_ref=mate_in.at[kind % 2], send_sem=a_send.at[kind % 2],
            recv_sem=a_recv.at[kind % 2], device_id=mate, device_id_type=MESH,
        )

    me = chip * 2 + x_lo

    def reduce_plane(owner):
        for h in range(2):
            to_owner(2 * owner + h).wait_recv()
        largest = None
        for h in range(2):
            for pos in range(CHIPS):
                for lo in range(2):
                    total = part[2 * owner + h, pos, lo] + mate_in[h, pos, lo]
                    mate_in[h, pos, lo] = total
                    size = jnp.max(jnp.abs(total).reshape(HALF // 8, 8, LANES), axis=0)
                    largest = size if largest is None else jnp.maximum(largest, size)
        exponent = exponent_of(jnp.max(largest, axis=0, keepdims=True))
        for pos in range(CHIPS):
            for lo in range(2):
                for h in range(2):
                    pair[2 * pos + lo, h * HALF : (h + 1) * HALF] = encode(mate_in[h, pos, lo], exponent)
                pair[2 * pos + lo, LAT:] = stamp(exponent)
        for k, (reg, pos, lo) in enumerate(plane):
            pltpu.make_async_remote_copy(
                src_ref=pair.at[pos * 2 + lo], dst_ref=plane_in.at[me], send_sem=b_send.at[k],
                recv_sem=b_recv.at[me], device_id=(reg, pos * 2 + core), device_id_type=MESH,
            ).start()
        plane_in[me] = pair[me]

    def early():
        @pl.when(core == 1)
        def _():
            reduce_plane(1)

    chunk(0, {2: lambda: pass_on(1 - core)})
    from_mate(core)
    rotate(2)
    rotate(1)
    chunk(3, {})
    advance(3)

    @pl.when(core == 0)
    def _():
        to_owner(3).start()

    chunk(2, {})
    advance(2)

    @pl.when(core == 0)
    def _():
        to_owner(2).start()

    chunk(1, {3: early})
    advance(1)
    advance(0)

    @pl.when(core == 1)
    def _():
        to_owner(1).start()
        to_owner(0).start()

    write = [pltpu.make_async_copy(grad_load, out_load, out_sem.at[0])]
    write[0].start()

    @pl.when(core == 0)
    def _():
        reduce_plane(0)

    grad_bias[...] = jnp.sum(jnp.transpose(bias_sum[...]), axis=0, keepdims=True)
    write.append(pltpu.make_async_copy(grad_bias, out_bias, out_sem.at[1]))
    write[1].start()

    for _, pos, lo in plane:
        pltpu.make_async_copy(pair.at[0], plane_in.at[pos * 2 + lo], b_recv.at[pos * 2 + lo]).wait()
    total = decode(plane_in, 0)
    for k in range(1, 2 * CHIPS):
        total = total + decode(plane_in, k)
    exponent = exponent_of(jnp.max(jnp.abs(total), axis=0, keepdims=True))
    mine[:LAT] = encode(total, exponent)
    mine[LAT:] = stamp(exponent)
    for k, (pz, lo) in enumerate(spread):
        copy = pltpu.make_async_remote_copy(
            src_ref=mine, dst_ref=final_in.at[region], send_sem=c_send.at[k],
            recv_sem=c_recv.at[region], device_id=(pz * 2 + lo, neuron), device_id_type=MESH,
        )
        copy.start()
        sends.append(copy)
    final_in[region] = mine[...]
    for k in range(2):
        to_owner(k).wait_send()
    for k in range(len(plane)):
        pltpu.make_async_copy(pair.at[0], plane_in.at[0], b_send.at[k]).wait()
    for pz, lo in spread:
        pltpu.make_async_copy(mine, final_in.at[pz * 2 + lo], c_recv.at[pz * 2 + lo]).wait()
    for lo in range(2):
        total = decode(final_in, lo)
        for k in range(1, 8):
            total = total + decode(final_in, 2 * k + lo)
        for h in range(2):
            grad_lat[lo * HALF : (lo + 1) * HALF, h * LANES : (h + 1) * LANES] = total[h * HALF : (h + 1) * HALF]
    write.append(pltpu.make_async_copy(grad_lat, out_lat, out_sem.at[2]))
    write[2].start()
    for copy in write:
        copy.wait()
    for copy in sends:
        copy.wait_send()


def hand_over(lat_in, load_in, bias_in, lat_out, load_out, bias_out):
    lat_out[...] = lat_in[...]
    load_out[...] = load_in[...]
    bias_out[...] = bias_in[...]


def per_device(counts, latents, loadings, bias, delays, recorded):
    vmem = pl.BlockSpec(memory_space=pltpu.VMEM)
    anywhere = pl.BlockSpec(memory_space=pl.ANY)
    shapes = (
        jax.ShapeDtypeStruct((LAT, 2 * LANES), F32),
        jax.ShapeDtypeStruct((LAT, NEU), F32),
        jax.ShapeDtypeStruct((1, NEU), F32),
    )
    dma = pltpu.SemaphoreType.DMA
    results = pl.pallas_call(
        kernel,
        out_shape=shapes,
        in_specs=[anywhere] * 5 + [vmem],
        out_specs=(anywhere,) * 3,
        scratch_shapes=[
            pltpu.VMEM((NEU, TIME), BF16),
            pltpu.VMEM((LAT, NEU), BF16),
            pltpu.VMEM((1, NEU), F32),
            pltpu.VMEM((1, LAT), jnp.int32),
            pltpu.VMEM((2, 2, CHIPS, LAT, LANES), BF16),
            pltpu.VMEM((TILES + 1, LAT, LANES), F32),
            pltpu.VMEM((4, DEPTH, CHUNK), BF16),
            pltpu.VMEM((NEU, DEPTH), BF16),
            pltpu.VMEM((NEU, LANES), F32),
            pltpu.VMEM((TILES + 1, LAT, LANES), F32),
            pltpu.VMEM((4, CHIPS, 2, HALF, LANES), F32),
            pltpu.VMEM((2, CHIPS, 2, HALF, LANES), F32),
            pltpu.VMEM((2 * CHIPS, CODED, LANES), I16),
            pltpu.VMEM((2 * CHIPS, CODED, LANES), I16),
            pltpu.VMEM((CODED, LANES), I16),
            pltpu.VMEM((16, CODED, LANES), I16),
            pltpu.VMEM((LAT, 2 * LANES), F32),
            pltpu.VMEM((LAT, NEU), F32),
            pltpu.VMEM((1, NEU), F32),
            dma((5,)),
            dma((ROWS,)),
            dma((2, CHIPS)),
            dma((2, CHIPS)),
            dma((2, CHIPS)),
            dma((2, CHIPS)),
            dma((2,)),
            dma((2,)),
            dma((15,)),
            dma((16,)),
            dma((15,)),
            dma((16,)),
            dma((3,)),
        ],
        compiler_params=pltpu.CompilerParams(
            collective_id=0, has_side_effects=True, vmem_limit_bytes=58 * 2**20
        ),
    )(counts[0], latents, loadings[0], bias, delays, recorded)
    grad_lat, grad_load, grad_bias = pl.pallas_call(
        hand_over,
        out_shape=shapes,
        in_specs=[vmem] * 3,
        out_specs=(vmem,) * 3,
    )(*results)
    return grad_lat, grad_load[None], grad_bias


def solution(mesh):
    placed = (
        P("region", "neuron", None),
        P(None, "neuron"),
        P("region", None, "neuron"),
        P("region", "neuron"),
        P("region", None),
        P("region"),
    )
    return jax.shard_map(
        per_device,
        mesh=mesh,
        in_specs=placed,
        out_specs=(P(None, "neuron"), P("region", None, "neuron"), P("region", "neuron")),
        check_vma=False,
    )
```

```python
import functools

import jax
import jax.numpy as jnp
from jax import lax
from jax.experimental import pallas as pl
from jax.experimental.pallas import tpu as pltpu
from jax.sharding import PartitionSpec as P

MESH = pl.DeviceIdType.MESH
LANES = 128
LAT = 64
HALF = LAT // 2
NEU = 1280
TIME = 4096
TILES = TIME // LANES
CHIPS = 8
CHUNK = CHIPS * LANES
DEPTH = 128
ROWS = 4
BLOCK = 256
CODED = LAT + 16
BITS = 14
NEAR = ((0, 1), (0, 3), (1, 0), (0, 2), (1, 1), (1, 3), (1, 2))
F32 = jnp.float32
BF16 = jnp.bfloat16
I16 = jnp.int16


def split_three(value):
    high = value.astype(BF16)
    rest = value - high.astype(F32)
    middle = rest.astype(BF16)
    return high.astype(F32), middle.astype(F32), rest - middle.astype(F32)


def exponent_of(largest):
    return jnp.floor(jnp.log2(jnp.maximum(largest, 1e-30))) + 1.0


def encode(value, exponent):
    return jnp.round(value * jnp.exp2(BITS - exponent)).astype(jnp.int32).astype(I16)


def stamp(exponent):
    return jnp.broadcast_to(exponent, (CODED - LAT, LANES)).astype(jnp.int32).astype(I16)


def decode(ref, *index):
    whole = ref[index].astype(jnp.int32).astype(F32)
    return whole[:LAT] * jnp.exp2(whole[LAT : LAT + 1] - BITS)


def kernel(
    counts_hbm, lat_hbm, load_hbm, bias_hbm, delay_hbm, rec_ref,
    grad_lat, grad_load, grad_bias,
    counts, load_ref, bias_ref, delay_ref, latb, rot, piece, load_t, bias_sum, spun, part, mate_in, pair, plane_in,
    mine, final_in,
    in_sem, cnt_sem, ag_send, ag_recv, fw_send, fw_recv, a_send, a_recv, b_send, b_recv, c_send, c_recv,
):
    region = lax.axis_index("region")
    neuron = lax.axis_index("neuron")
    z, x_lo = region // 2, region % 2
    x_hi, y, core = neuron // 8, (neuron // 2) % 4, neuron % 2
    chip = neuron // 2
    x = x_hi * 2 + x_lo
    mate = (region, chip * 2 + 1 - core)

    plane = []
    for dx in range(4):
        for dy in range(4):
            if (dx, dy) != (0, 0):
                px, py = (x + dx) % 4, (y + dy) % 4
                plane.append(((z * 2 + px % 2), (px // 2) * 4 + py, px % 2))
    spread = []
    for dz in (0, 4, 3, 5, 2, 6, 1, 7):
        for dl in (1, 0):
            if (dz, dl) != (0, 0):
                spread.append((((z + dz) % 8), (x_lo + dl) % 2))

    barrier = pltpu.get_barrier_semaphore()
    for pz, lo in spread[1:]:
        pl.semaphore_signal(barrier, inc=1, device_id=(pz * 2 + lo, neuron), device_id_type=MESH)
    for reg, pos, _ in plane:
        pl.semaphore_signal(barrier, inc=1, device_id=(reg, pos * 2 + core), device_id_type=MESH)
    pl.semaphore_signal(barrier, inc=1, device_id=mate, device_id_type=MESH)

    own = []
    for h in range(2):
        copy = pltpu.make_async_copy(
            lat_hbm.at[:, pl.ds(h * LANES, LANES)], latb.at[core, h, chip], in_sem.at[h]
        )
        copy.start()
        own.append(copy)
    smalls = []
    for k, (source, target) in enumerate(((load_hbm, load_ref), (bias_hbm, bias_ref), (delay_hbm, delay_ref))):
        copy = pltpu.make_async_copy(source, target, in_sem.at[2 + k])
        copy.start()
        smalls.append(copy)
    block = NEU // ROWS
    loads = []
    for k in range(ROWS):
        rows = pl.ds(k * block, block)
        copy = pltpu.make_async_copy(counts_hbm.at[rows], counts.at[rows], cnt_sem.at[k])
        copy.start()
        loads.append(copy)

    for copy in own:
        copy.wait()
    pl.semaphore_wait(barrier, 1 + len(plane) + len(spread) - 1)
    sends = []

    def to_mate(h, pos):
        copy = pltpu.make_async_remote_copy(
            src_ref=latb.at[core, h, pos], dst_ref=latb.at[core, h, pos], send_sem=fw_send.at[h, pos],
            recv_sem=fw_recv.at[h, pos], device_id=mate, device_id_type=MESH,
        )
        copy.start()
        sends.append(copy)

    arrivals = []
    for h in (core, 1 - core):
        for dxh, dy in NEAR:
            px = 3 - x if dxh else x
            pos = (px // 2) * 4 + (y + dy) % 4
            copy = pltpu.make_async_remote_copy(
                src_ref=latb.at[core, h, chip], dst_ref=latb.at[core, h, chip], send_sem=ag_send.at[h, pos],
                recv_sem=ag_recv.at[h, chip], device_id=(z * 2 + px % 2, pos * 2 + core), device_id_type=MESH,
            )
            copy.start()
            sends.append(copy)
            if len(arrivals) < CHIPS - 1:
                arrivals.append(pos)
        to_mate(h, chip)

    for copy in smalls:
        copy.wait()
    ba, bb, bc = split_three(bias_ref[...])
    stacked = jnp.concatenate([load_ref[...].astype(F32), ba, bb, bc, jnp.zeros((DEPTH - LAT - 3, NEU), F32)], axis=0)
    load_t[...] = jnp.transpose(stacked).astype(BF16)
    tail = lax.broadcasted_iota(jnp.int32, (DEPTH - LAT, CHUNK), 0)
    for kind in range(4):
        piece[kind, LAT:] = jnp.where(tail < 3, 1.0, 0.0).astype(BF16)
    grad_load[...] = jnp.zeros_like(grad_load)
    bias_sum[...] = jnp.zeros_like(bias_sum)
    rot[0] = jnp.zeros((LAT, LANES), F32)
    spun[TILES] = jnp.zeros((LAT, LANES), F32)
    same = lax.broadcasted_iota(jnp.int32, (LAT, LAT), 0) == lax.broadcasted_iota(jnp.int32, (LAT, LAT), 1)
    delay = jnp.sum(jnp.where(same, delay_ref[...].astype(F32), 0.0), axis=1, keepdims=True).astype(jnp.int32)
    lane = lax.broadcasted_iota(jnp.int32, (LAT, LANES), 1)
    back = (lane - delay) & (LANES - 1)
    ahead = (lane + delay) & (LANES - 1)
    kept = lane >= delay
    near = lane + delay < LANES
    recorded = rec_ref[...].reshape(1, 1)

    def pass_on(h):
        for pos in arrivals:
            pltpu.make_async_copy(latb.at[core, h, chip], latb.at[core, h, pos], ag_recv.at[h, pos]).wait()
            to_mate(h, pos)

    def from_mate(h):
        for pos in [chip] + arrivals:
            pltpu.make_async_copy(latb.at[core, h, chip], latb.at[1 - core, h, pos], fw_recv.at[h, pos]).wait()

    def rotate(kind):
        for pos in range(CHIPS):
            source = latb[kind // 2, kind % 2, pos].astype(F32)
            rot[pos * 4 + kind + 1] = jnp.take_along_axis(source, back, axis=1)

    pass_on(core)
    from_mate(1 - core)
    rotate(0)
    rotate(3)
    for copy in loads:
        copy.wait()

    def chunk(kind, between):
        for pos in range(CHIPS):
            tile = pos * 4 + kind
            piece[kind, :LAT, pos * LANES : (pos + 1) * LANES] = jnp.where(kept, rot[tile + 1], rot[tile]).astype(BF16)
        bins = lax.broadcasted_iota(jnp.int32, (1, CHUNK), 1)
        bins = (bins // LANES) * (4 * LANES) + kind * LANES + bins % LANES
        live = bins < recorded
        shift = None
        for k in range(NEU // BLOCK):
            if k in between:
                between[k]()
            rows = slice(k * BLOCK, (k + 1) * BLOCK)
            eta = jnp.dot(load_t[rows], piece[kind], preferred_element_type=F32)
            observed = jnp.concatenate(
                [counts[rows, (pos * 4 + kind) * LANES : (pos * 4 + kind + 1) * LANES] for pos in range(CHIPS)], axis=1
            )
            resid = jnp.where(live, jnp.exp(eta) - observed.astype(F32), 0.0)
            total = resid[:, :LANES]
            for pos in range(1, CHIPS):
                total = total + resid[:, pos * LANES : (pos + 1) * LANES]
            bias_sum[rows] += total
            low = resid.astype(BF16)
            grad_load[:, rows] += lax.dot_general(
                piece[kind, :LAT], low, (((1,), (1,)), ((), ())), preferred_element_type=F32
            )
            part_shift = jnp.dot(load_ref[:, rows], low, preferred_element_type=F32)
            shift = part_shift if shift is None else shift + part_shift
        for pos in range(CHIPS):
            spun[pos * 4 + kind] = jnp.take_along_axis(shift[:, pos * LANES : (pos + 1) * LANES], ahead, axis=1)

    def advance(kind):
        for pos in range(CHIPS):
            tile = pos * 4 + kind
            moved = jnp.where(near, spun[tile], spun[tile + 1])
            part[kind, pos, 0] = moved[:HALF]
            part[kind, pos, 1] = moved[HALF:]

    def to_owner(kind):
        return pltpu.make_async_remote_copy(
            src_ref=part.at[kind], dst_ref=mate_in.at[kind % 2], send_sem=a_send.at[kind % 2],
            recv_sem=a_recv.at[kind % 2], device_id=mate, device_id_type=MESH,
        )

    me = chip * 2 + x_lo

    def reduce_plane(owner):
        largest = None
        for h in (1, 0):
            to_owner(2 * owner + h).wait_recv()
            for pos in range(CHIPS):
                for lo in range(2):
                    total = part[2 * owner + h, pos, lo] + mate_in[h, pos, lo]
                    mate_in[h, pos, lo] = total
                    size = jnp.max(jnp.abs(total).reshape(HALF // 8, 8, LANES), axis=0)
                    largest = size if largest is None else jnp.maximum(largest, size)
        exponent = exponent_of(jnp.max(largest, axis=0, keepdims=True))
        for pos in range(CHIPS):
            for lo in range(2):
                for h in range(2):
                    pair[2 * pos + lo, h * HALF : (h + 1) * HALF] = encode(mate_in[h, pos, lo], exponent)
                pair[2 * pos + lo, LAT:] = stamp(exponent)
        for k, (reg, pos, lo) in enumerate(plane):
            pltpu.make_async_remote_copy(
                src_ref=pair.at[pos * 2 + lo], dst_ref=plane_in.at[me], send_sem=b_send.at[k],
                recv_sem=b_recv.at[me], device_id=(reg, pos * 2 + core), device_id_type=MESH,
            ).start()
        plane_in[me] = pair[me]

    def early():
        @pl.when(core == 1)
        def _():
            reduce_plane(1)

    chunk(0, {2: lambda: pass_on(1 - core)})
    from_mate(core)
    rotate(2)
    rotate(1)
    chunk(3, {})
    advance(3)

    @pl.when(core == 0)
    def _():
        to_owner(3).start()

    chunk(2, {})
    advance(2)

    @pl.when(core == 0)
    def _():
        to_owner(2).start()

    chunk(1, {3: early})
    advance(1)

    @pl.when(core == 1)
    def _():
        to_owner(1).start()

    advance(0)

    @pl.when(core == 1)
    def _():
        to_owner(0).start()

    @pl.when(core == 0)
    def _():
        reduce_plane(0)

    grad_bias[...] = jnp.sum(jnp.transpose(bias_sum[...]), axis=0, keepdims=True)

    for _, pos, lo in plane:
        pltpu.make_async_copy(pair.at[0], plane_in.at[pos * 2 + lo], b_recv.at[pos * 2 + lo]).wait()
    total = decode(plane_in, 0)
    for k in range(1, 2 * CHIPS):
        total = total + decode(plane_in, k)
    exponent = exponent_of(jnp.max(jnp.abs(total), axis=0, keepdims=True))
    mine[:LAT] = encode(total, exponent)
    mine[LAT:] = stamp(exponent)
    for k, (pz, lo) in enumerate(spread):
        copy = pltpu.make_async_remote_copy(
            src_ref=mine, dst_ref=final_in.at[region], send_sem=c_send.at[k],
            recv_sem=c_recv.at[region], device_id=(pz * 2 + lo, neuron), device_id_type=MESH,
        )
        copy.start()
        sends.append(copy)
    final_in[region] = mine[...]
    for k in range(2):
        to_owner(k).wait_send()
    for k in range(len(plane)):
        pltpu.make_async_copy(pair.at[0], plane_in.at[0], b_send.at[k]).wait()
    for pz, lo in spread:
        pltpu.make_async_copy(mine, final_in.at[pz * 2 + lo], c_recv.at[pz * 2 + lo]).wait()
    for lo in range(2):
        total = decode(final_in, lo)
        for k in range(1, 8):
            total = total + decode(final_in, 2 * k + lo)
        for h in range(2):
            grad_lat[lo * HALF : (lo + 1) * HALF, h * LANES : (h + 1) * LANES] = total[h * HALF : (h + 1) * HALF]
    for copy in sends:
        copy.wait_send()


def hand_over(lat_in, load_in, bias_in, lat_out, load_out, bias_out):
    lat_out[...] = lat_in[...]
    load_out[...] = load_in[...]
    bias_out[...] = bias_in[...]


def per_device(counts, latents, loadings, bias, delays, recorded):
    vmem = pl.BlockSpec(memory_space=pltpu.VMEM)
    anywhere = pl.BlockSpec(memory_space=pl.ANY)
    shapes = (
        jax.ShapeDtypeStruct((LAT, 2 * LANES), F32),
        jax.ShapeDtypeStruct((LAT, NEU), F32),
        jax.ShapeDtypeStruct((1, NEU), F32),
    )
    dma = pltpu.SemaphoreType.DMA
    results = pl.pallas_call(
        kernel,
        out_shape=tuple(pltpu.VMEM(part.shape, part.dtype) for part in shapes),
        in_specs=[anywhere] * 5 + [vmem],
        out_specs=(vmem,) * 3,
        scratch_shapes=[
            pltpu.VMEM((NEU, TIME), BF16),
            pltpu.VMEM((LAT, NEU), BF16),
            pltpu.VMEM((1, NEU), F32),
            pltpu.VMEM((1, LAT), jnp.int32),
            pltpu.VMEM((2, 2, CHIPS, LAT, LANES), BF16),
            pltpu.VMEM((TILES + 1, LAT, LANES), F32),
            pltpu.VMEM((4, DEPTH, CHUNK), BF16),
            pltpu.VMEM((NEU, DEPTH), BF16),
            pltpu.VMEM((NEU, LANES), F32),
            pltpu.VMEM((TILES + 1, LAT, LANES), F32),
            pltpu.VMEM((4, CHIPS, 2, HALF, LANES), F32),
            pltpu.VMEM((2, CHIPS, 2, HALF, LANES), F32),
            pltpu.VMEM((2 * CHIPS, CODED, LANES), I16),
            pltpu.VMEM((2 * CHIPS, CODED, LANES), I16),
            pltpu.VMEM((CODED, LANES), I16),
            pltpu.VMEM((16, CODED, LANES), I16),
            dma((5,)),
            dma((ROWS,)),
            dma((2, CHIPS)),
            dma((2, CHIPS)),
            dma((2, CHIPS)),
            dma((2, CHIPS)),
            dma((2,)),
            dma((2,)),
            dma((15,)),
            dma((16,)),
            dma((15,)),
            dma((16,)),
        ],
        compiler_params=pltpu.CompilerParams(
            collective_id=0, has_side_effects=True, vmem_limit_bytes=58 * 2**20
        ),
    )(counts[0], latents, loadings[0], bias, delays, recorded)
    grad_lat, grad_load, grad_bias = pl.pallas_call(
        hand_over,
        out_shape=shapes,
        in_specs=[vmem] * 3,
        out_specs=(vmem,) * 3,
    )(*[pltpu.with_memory_space_constraint(part, pltpu.VMEM) for part in results])
    return grad_lat, grad_load[None], grad_bias


def solution(mesh):
    placed = (
        P("region", "neuron", None),
        P(None, "neuron"),
        P("region", None, "neuron"),
        P("region", "neuron"),
        P("region", None),
        P("region"),
    )
    return jax.shard_map(
        per_device,
        mesh=mesh,
        in_specs=placed,
        out_specs=(P(None, "neuron"), P("region", None, "neuron"), P("region", "neuron")),
        check_vma=False,
    )
```
